32 devices in a mesh: group: 4 (over x, core), seq: 8 (over z, y).
Axes of the slice: x: 2, y: 2, z: 4, core: 2. Of those that a mesh axis runs over, the one named last changes fastest.
Arguments:
- prefill_query: bfloat16 [4, 512, 8192], P('group', 'seq'), may hold values from -40 to 40
- prefill_key: bfloat16 [4, 512, 1024], P('group', 'seq'), may hold values from -40 to 40
- prefill_value: bfloat16 [4, 512, 1024], P('group', 'seq'), may hold values from -6 to 6
- lengths: int32 [4], replicated, may hold values from 128 to 512
- verify_query: bfloat16 [64, 4, 8192], P(('group', 'seq')), may hold values from -40 to 40
- verify_key: bfloat16 [64, 4, 1024], P(('group', 'seq')), may hold values from -6 to 6
- verify_value: bfloat16 [64, 4, 1024], P(('group', 'seq')), may hold values from -6 to 6
- owner: int32 [64], replicated, may hold values from 0 to 3
- cached: int32 [64], replicated, may hold values from 1 to 8
Outputs:
- prefill_out: bfloat16 [4, 512, 8192], P('group', 'seq')
- verify_out: bfloat16 [64, 4, 8192], P(('group', 'seq'))
The draws below stay inside these ranges and needn't reach their ends.
All inputs are finite; a program needn't handle non-finite values.
Results may differ from the reference program's by a relative error of at most 0.005.
Values may be sent and summed in bfloat16 or wider, within the bound.
A program may use at most 192 MiB of HBM per device.

```python
import math
import jax
import jax.numpy as jnp
from jax import lax

HQ = 64
HK = 8
HD = 128
STEPS = 4
BLK = 64
TOK_DEV = 64
TRAJ = 4
LENGTH = 512
ROWS = 64
N_GROUP = 4
N_SEQ = 8


def draw_prefill_query(key, part):
    values = jax.random.truncated_normal(jax.random.fold_in(key, 21), -6.0, 6.0, (TRAJ, LENGTH, HQ * HD), jnp.float32)
    return values.astype(jnp.bfloat16)


def draw_prefill_key(key, part):
    values = jax.random.truncated_normal(jax.random.fold_in(key, 22), -6.0, 6.0, (TRAJ, LENGTH, HK * HD), jnp.float32)
    return values.astype(jnp.bfloat16)


def draw_verify_query(key, part):
    values = jax.random.truncated_normal(jax.random.fold_in(key, 24), -6.0, 6.0, (ROWS, STEPS, HQ * HD), jnp.float32)
    return values.astype(jnp.bfloat16)


def touch_ends(values, key, smallest, top_value):
    longest = values.shape.index(max(values.shape))
    spots = []
    for shift in (0, 1):
        where = [jax.random.randint(jax.random.fold_in(key, axis), (), 0, length) for axis, length in enumerate(values.shape)]
        where[longest] = (where[longest] + shift) % values.shape[longest]
        spots.append(tuple(where))
    return values.at[spots[0]].set(smallest).at[spots[1]].set(top_value)


def block_scale(own_key, shape, cuts, least, top_value):
    def one(axis_at, blocks):
        heights = jax.random.uniform(jax.random.fold_in(jax.random.fold_in(own_key, 6), axis_at), (blocks,), jnp.float32, least / len(cuts), top_value / len(cuts))
        return jnp.repeat(jnp.exp(heights), shape[axis_at] // blocks).reshape((-1,) + (1,) * (len(shape) - axis_at - 1))

    factor_of = one(*cuts[0])
    for cut in cuts[1:]:
        factor_of = factor_of * one(*cut)
    return factor_of


def scatter_about(key, dims, scale, reach, shards=(), kind=jnp.bfloat16):
    entries = jax.random.normal(key, dims, jnp.float32) * scale
    if len(shards) > 0:
        entries = block_scale(key, dims, shards, -0.22, 0.18) * entries
    return jnp.clip(entries, min=-reach, max=reach).astype(kind)


def setup_inputs(seed: int = 0) -> dict:
    splits = jax.random.split(jax.random.key(seed), 10)
    return {
        "prefill_query": draw_prefill_query(jax.random.fold_in(splits[9], 71), 0),
        "prefill_key": draw_prefill_key(jax.random.fold_in(splits[9], 71), 0),
        "prefill_value": scatter_about(splits[2], (TRAJ, LENGTH, HK * HD), 1.0, 6.0, ((0, 4), (1, 8))),
        "lengths": touch_ends(jax.random.randint(splits[3], (TRAJ,), TOK_DEV * N_SEQ // 4, TOK_DEV * N_SEQ + 1), jax.random.fold_in(splits[3], 1), TOK_DEV * N_SEQ // 4, TOK_DEV * N_SEQ).astype(jnp.int32),
        "verify_query": draw_verify_query(jax.random.fold_in(splits[9], 71), 0),
        "verify_key": scatter_about(splits[5], (ROWS, STEPS, HK * HD), 1.0, 6.0, ((0, 32),)),
        "verify_value": scatter_about(splits[6], (ROWS, STEPS, HK * HD), 1.0, 6.0, ((0, 32),)),
        "owner": touch_ends(jax.random.randint(splits[7], (ROWS,), 0, N_GROUP), jax.random.fold_in(splits[7], 1), 0, N_GROUP - 1).astype(jnp.int32),
        "cached": touch_ends(jax.random.randint(splits[8], (ROWS,), 1, TOK_DEV * N_SEQ // BLK + 1), jax.random.fold_in(splits[8], 1), 1, (TOK_DEV * N_SEQ // BLK + 1) - 1).astype(jnp.int32),
    }


def prefill_part(query_one, key_one, value_one, length):
    block = math.gcd(LENGTH, 256)
    group = HQ // HK
    scale = HD ** -0.5
    keys = key_one.reshape(LENGTH, HK, HD).astype(jnp.float32)
    values = value_one.reshape(LENGTH, HK, HD).astype(jnp.float32)
    queries = query_one.reshape(LENGTH // block, block, HK, group, HD)
    starts = jnp.arange(LENGTH // block, dtype=jnp.int32) * block

    def one_block(inputs):
        query_block, start = inputs
        scores = jnp.einsum("tkgd,jkd->tkgj", query_block.astype(jnp.float32), keys) * scale
        slots = start + jnp.arange(block, dtype=jnp.int32)
        columns = jnp.arange(LENGTH, dtype=jnp.int32)
        allowed = (columns[None, :] <= slots[:, None]) & (columns[None, :] < length)
        allowed = allowed[:, None, None, :]
        masked = jnp.where(allowed, scores, -1e30)
        highest = jnp.max(masked, axis=-1, keepdims=True)
        weights = jnp.where(allowed, jnp.exp(scores - highest), 0.0)
        summed = jnp.sum(weights, axis=-1)
        rounded = lax.optimization_barrier(weights.astype(jnp.bfloat16))
        mixed = jnp.einsum("tkgj,jkd->tkgd", rounded.astype(jnp.float32), values)
        return (mixed / summed[..., None]).astype(jnp.bfloat16).reshape(block, HQ * HD)

    return lax.map(one_block, (queries, starts)).reshape(LENGTH, HQ * HD)


def reference(prefill_query, prefill_key, prefill_value, lengths, verify_query, verify_key, verify_value, owner, cached):
    prefill_out = lax.map(lambda inputs: prefill_part(*inputs), (prefill_query, prefill_key, prefill_value, lengths))
    group = HQ // HK
    scale = HD ** -0.5
    row_block = math.gcd(ROWS, 8)
    blocks = ROWS // row_block
    queries = verify_query.reshape(blocks, row_block, STEPS, HK, group, HD)
    fresh_keys = verify_key.reshape(blocks, row_block, STEPS, HK, HD)
    fresh_values = verify_value.reshape(blocks, row_block, STEPS, HK, HD)
    limits = jnp.minimum(cached * BLK, lengths[owner]).astype(jnp.int32).reshape(blocks, row_block)
    owners = owner.reshape(blocks, row_block)
    cache_keys = prefill_key.reshape(TRAJ, LENGTH, HK, HD)
    cache_values = prefill_value.reshape(TRAJ, LENGTH, HK, HD)
    steps_order = jnp.arange(STEPS, dtype=jnp.int32)
    causal = (steps_order[None, :] <= steps_order[:, None])[None, :, None, None, :]

    def one_block(inputs):
        query_block, key_block, value_block, owner_block, limit_block = inputs
        row_keys = cache_keys[owner_block].astype(jnp.float32)
        row_values = cache_values[owner_block].astype(jnp.float32)
        query_wide = query_block.astype(jnp.float32)
        scores = jnp.einsum("rtkgd,rjkd->rtkgj", query_wide, row_keys) * scale
        columns = jnp.arange(LENGTH, dtype=jnp.int32)
        allowed = (columns[None, :] < limit_block[:, None])[:, None, None, None, :]
        fresh = jnp.einsum("rtkgd,rskd->rtkgs", query_wide, key_block.astype(jnp.float32)) * scale
        highest = jnp.maximum(jnp.max(jnp.where(allowed, scores, -1e30), axis=-1), jnp.max(jnp.where(causal, fresh, -1e30), axis=-1))
        weights = jnp.where(allowed, jnp.exp(scores - highest[..., None]), 0.0)
        fresh_weights = jnp.where(causal, jnp.exp(fresh - highest[..., None]), 0.0)
        summed = jnp.sum(weights, axis=-1) + jnp.sum(fresh_weights, axis=-1)
        rounded = lax.optimization_barrier(weights.astype(jnp.bfloat16))
        fresh_rounded = lax.optimization_barrier(fresh_weights.astype(jnp.bfloat16))
        mixed = jnp.einsum("rtkgj,rjkd->rtkgd", rounded.astype(jnp.float32), row_values)
        mixed = mixed + jnp.einsum("rtkgs,rskd->rtkgd", fresh_rounded.astype(jnp.float32), value_block.astype(jnp.float32))
        return (mixed / summed[..., None]).astype(jnp.bfloat16).reshape(row_block, STEPS, HQ * HD)

    verify_out = lax.map(one_block, (queries, fresh_keys, fresh_values, owners, limits)).reshape(ROWS, STEPS, HQ * HD)
    return prefill_out, verify_out
```

```python
import functools
import math

import jax
import jax.numpy as jnp
from jax import lax
from jax.experimental import pallas as pl
from jax.experimental.pallas import tpu as pltpu
from jax.sharding import PartitionSpec as P

HQ = 64
HK = 8
HD = 128
BLK = 64
PIECES = 4
LOW = -1e30
MESH = pl.DeviceIdType.MESH
FACTOR = HD ** (-0.5) * math.log2(math.e)


def dot_t(a, b):
    return lax.dot_general(a, b, (((1,), (1,)), ((), ())), preferred_element_type=jnp.float32)


def kernel(
    cycle, trajs, lengths, owner, cached, pq, pk, pv, vq, vk, vv, pout, vout,
    kvbuf, cache, qsend, qland, osend, oland, bias,
    q_send, q_recv, c_send, c_recv, g_send, g_recv, z_send, z_recv, y_send, y_recv, o_send, o_recv,
):
    g = lax.axis_index("group")
    s = lax.axis_index("seq")
    tokens = pq.shape[1]
    local_rows, steps = vq.shape[0], vq.shape[1]
    rows = local_rows * steps
    slots = cycle * tokens
    own_heads = HQ // cycle
    per_head = cycle // HK
    width = own_heads * HD
    row_count = local_rows * cycle
    group = HQ // HK
    chain = cycle // 2
    z = s // 2
    y = s % 2
    heads = HK // PIECES

    barrier = pltpu.get_barrier_semaphore()

    def greet(i, carry):
        pl.semaphore_signal(barrier, inc=1, device_id=(g, lax.rem(s + i, cycle)), device_id_type=MESH)
        return carry

    lax.fori_loop(1, cycle, greet, 0)
    for i in range(1, trajs):
        pl.semaphore_signal(barrier, inc=1, device_id=(lax.rem(g + i, trajs), s), device_id_type=MESH)

    def span(t):
        return pl.ds(pl.multiple_of(t * tokens, tokens), tokens)

    mine = span(s)
    for k in range(HK):
        kvbuf[k, mine, 0:HD] = pk[0, :, k * HD : (k + 1) * HD]
        kvbuf[k, mine, HD : 2 * HD] = pv[0, :, k * HD : (k + 1) * HD]
    wide_q = jnp.concatenate([vq[r].astype(jnp.float32) for r in range(local_rows)], axis=0)
    wide_k = jnp.concatenate([vk[r].astype(jnp.float32) for r in range(local_rows)], axis=0)
    wide_v = jnp.concatenate([vv[r].astype(jnp.float32) for r in range(local_rows)], axis=0)
    for t in range(cycle):
        k = t // per_head
        qsend[t, :, 0:width] = wide_q[:, t * width : (t + 1) * width].astype(jnp.bfloat16)
        qsend[t, :, width : width + HD] = wide_k[:, k * HD : (k + 1) * HD].astype(jnp.bfloat16)
        qsend[t, :, width + HD : width + 2 * HD] = wide_v[:, k * HD : (k + 1) * HD].astype(jnp.bfloat16)
    pl.semaphore_wait(barrier, cycle - 1 + trajs - 1)

    def row_copy(to, source):
        return pltpu.make_async_remote_copy(
            src_ref=qsend.at[to], dst_ref=qland.at[source],
            send_sem=q_send.at[to], recv_sem=q_recv.at[source],
            device_id=(g, to), device_id_type=MESH,
        )

    def head_copy(to, source):
        return pltpu.make_async_remote_copy(
            src_ref=kvbuf.at[to // per_head, span(source)], dst_ref=cache.at[g, span(source)],
            send_sem=c_send.at[to], recv_sem=c_recv.at[source],
            device_id=(g, to), device_id_type=MESH,
        )

    def group_copy(to, traj, t):
        return pltpu.make_async_remote_copy(
            src_ref=cache.at[traj, span(t)], dst_ref=cache.at[traj, span(t)],
            send_sem=g_send.at[to, t], recv_sem=g_recv.at[traj, t],
            device_id=(to, s), device_id_type=MESH,
        )

    def piece(line, at, p):
        return kvbuf.at[pl.ds(p * heads, heads), span(2 * at + line)]

    def chain_copy(at, p):
        return pltpu.make_async_remote_copy(
            src_ref=piece(y, at, p), dst_ref=piece(y, at, p),
            send_sem=z_send.at[at, p], recv_sem=z_recv.at[at, p],
            device_id=(g, lax.rem(s + 2, cycle)), device_id_type=MESH,
        )

    def side_copy(line, at, p):
        return pltpu.make_async_remote_copy(
            src_ref=piece(line, at, p), dst_ref=piece(line, at, p),
            send_sem=y_send.at[at, p], recv_sem=y_recv.at[at, p],
            device_id=(g, s + 1 - 2 * y), device_id_type=MESH,
        )

    def out_copy(to, source):
        return pltpu.make_async_remote_copy(
            src_ref=osend.at[to], dst_ref=oland.at[source],
            send_sem=o_send.at[to], recv_sem=o_recv.at[source],
            device_id=(g, to), device_id_type=MESH,
        )

    def send_first(i, carry):
        to = lax.rem(s + i, cycle)
        head_copy(to, s).start()
        return carry

    lax.fori_loop(1, cycle, send_first, 0)

    def send_rows(i, carry):
        to = lax.rem(s + i, cycle)
        row_copy(to, s).start()
        return carry

    lax.fori_loop(1, cycle, send_rows, 0)
    for p in range(PIECES):
        @pl.when(z < chain - 1)
        def _():
            chain_copy(z, p).start()

        @pl.when(y == 0)
        def _():
            side_copy(y, z, p).start()

    cache[g, mine, :] = kvbuf[s // per_head, mine, :]
    qland[s] = qsend[s]
    for i in range(1, trajs):
        group_copy(lax.rem(g + i, trajs), g, s).start()

    def blank(t, carry):
        kvbuf[:, span(t), :] = jnp.zeros((HK, tokens, 2 * HD), jnp.bfloat16)
        return carry

    lax.fori_loop(s + 1, cycle, blank, 0)
    length = lengths[g]
    column = lax.broadcasted_iota(jnp.int32, (tokens, slots), 1)
    slot = s * tokens + lax.broadcasted_iota(jnp.int32, (tokens, slots), 0)
    bias[...] = jnp.where((column <= slot) & (column < length), 0.0, LOW)

    def pass_heads(i, carry):
        t = lax.rem(s + i, cycle)
        head_copy(s, t).wait_recv()
        for j in range(1, trajs):
            group_copy(lax.rem(g + j, trajs), g, t).start()
        return carry

    lax.fori_loop(1, cycle, pass_heads, 0)

    def forward(d, p):
        @pl.when(d <= z)
        def _():
            at = z - d
            chain_copy(at, p).wait_recv()

            @pl.when(z < chain - 1)
            def _():
                chain_copy(at, p).start()

            side_copy(y, at, p).start()

    def forward_all(low, high):
        def step(d, carry):
            for p in range(PIECES):
                forward(d, p)
            return carry

        lax.fori_loop(low, high, step, 0)

    def verify_one(t):
        wide = qland[t].astype(jnp.float32)
        queries = jnp.concatenate(
            [wide[:, h * HD : (h + 1) * HD] for h in range(own_heads)], axis=0
        ).astype(jnp.bfloat16)
        fresh_key = qland[t, :, width : width + HD]
        fresh_value = qland[t, :, width + HD : width + 2 * HD]
        count = own_heads * rows
        index = lax.broadcasted_iota(jnp.int32, (count, 1), 0) % rows
        row_of = index // steps
        where_to = lax.broadcasted_iota(jnp.int32, (count, slots), 1)
        scores = None
        owners = []
        for r in range(local_rows):
            row = g * row_count + t * local_rows + r
            who = owner[row]
            owners.append(who)
            limit = jnp.minimum(cached[row] * BLK, lengths[who])
            part = jnp.where(where_to < limit, dot_t(queries, cache[who, :, 0:HD]), LOW)
            scores = part if scores is None else jnp.where(row_of == r, part, scores)
        fresh_col = lax.broadcasted_iota(jnp.int32, (count, rows), 1)
        allowed = (fresh_col // steps == row_of) & (fresh_col % steps <= index % steps)
        fresh = jnp.where(allowed, dot_t(queries, fresh_key), LOW)
        highest = jnp.maximum(
            jnp.max(scores, axis=-1, keepdims=True), jnp.max(fresh, axis=-1, keepdims=True)
        )
        weights = jnp.exp2((scores - highest) * FACTOR)
        fresh_weights = jnp.exp2((fresh - highest) * FACTOR)
        total = jnp.sum(weights, axis=-1, keepdims=True) + jnp.sum(fresh_weights, axis=-1, keepdims=True)
        mixed = jnp.dot(
            fresh_weights.astype(jnp.bfloat16), fresh_value, preferred_element_type=jnp.float32
        )
        for r in range(local_rows):
            chosen = jnp.where(row_of == r, weights, 0.0).astype(jnp.bfloat16)
            mixed = mixed + jnp.dot(
                chosen, cache[owners[r], :, HD : 2 * HD], preferred_element_type=jnp.float32
            )
        result = (mixed / total).astype(jnp.bfloat16)
        for h in range(own_heads):
            osend[t, :, h * HD : (h + 1) * HD] = result[h * rows : (h + 1) * rows]

    def verify_some(low, high):
        def step(i, carry):
            t = lax.rem(s + i, cycle)
            verify_one(t)

            @pl.when(i > 0)
            def _():
                out_copy(t, s).start()

            return carry

        lax.fori_loop(low, high, step, 0)

    tile = max(1, min(group, (512 * 512) // (tokens * slots)))

    def attend(k, part):
        first = k * group + part * tile
        queries = jnp.concatenate(
            [pq[0, :, pl.ds(pl.multiple_of((first + h) * HD, HD), HD)] for h in range(tile)], axis=0
        )
        scores = dot_t(queries, kvbuf[k, :, 0:HD]).reshape(tile, tokens, slots) + bias[...][None]
        highest = jnp.max(scores, axis=-1, keepdims=True)
        weights = jnp.exp2((scores - highest) * FACTOR)
        total = jnp.sum(weights, axis=-1, keepdims=True)
        mixed = jnp.dot(
            weights.astype(jnp.bfloat16).reshape(tile * tokens, slots),
            kvbuf[k, :, HD : 2 * HD],
            preferred_element_type=jnp.float32,
        )
        result = (mixed / total.reshape(tile * tokens, 1)).astype(jnp.bfloat16)
        for h in range(tile):
            pout[0, :, pl.ds(pl.multiple_of((first + h) * HD, HD), HD)] = result[
                h * tokens : (h + 1) * tokens
            ]

    def prefill_piece(p):
        def wait_one(at, carry):
            side_copy(1 - y, at, p).wait_recv()
            return carry

        lax.fori_loop(0, z + y, wait_one, 0)

        def step(i, carry):
            attend(p * heads + i // (group // tile), i % (group // tile))
            return carry

        lax.fori_loop(0, heads * (group // tile), step, 0)

    forward_all(1, chain - 2)

    def rows_arrive(i, carry):
        row_copy(s, lax.rem(s + i, cycle)).wait_recv()
        return carry

    lax.fori_loop(1, cycle, rows_arrive, 0)

    def caches_arrive(t, carry):
        for i in range(1, trajs):
            group_copy(g, lax.rem(g + i, trajs), t).wait_recv()
        return carry

    lax.fori_loop(0, cycle, caches_arrive, 0)
    verify_some(1, cycle // 2)
    forward_all(chain - 2, chain - 1)
    verify_some(cycle // 2, cycle)
    verify_some(0, 1)
    oland[s] = osend[s]
    forward(chain - 1, 0)
    for p in range(PIECES):
        if p + 1 < PIECES:
            forward(chain - 1, p + 1)
        prefill_piece(p)

    def outs_arrive(i, carry):
        out_copy(s, lax.rem(s + i, cycle)).wait_recv()
        return carry

    lax.fori_loop(1, cycle, outs_arrive, 0)
    for t in range(cycle):
        block = oland[t].astype(jnp.float32)
        for r in range(local_rows):
            vout[r, :, t * width : (t + 1) * width] = block[r * steps : (r + 1) * steps].astype(
                jnp.bfloat16
            )

    def left(i, carry):
        to = lax.rem(s + i, cycle)
        head_copy(to, s).wait_send()
        row_copy(to, s).wait_send()
        out_copy(to, s).wait_send()
        return carry

    lax.fori_loop(1, cycle, left, 0)

    def left_group(t, carry):
        for i in range(1, trajs):
            group_copy(lax.rem(g + i, trajs), g, t).wait_send()
        return carry

    lax.fori_loop(0, cycle, left_group, 0)

    @pl.when(z < chain - 1)
    def _():
        def step(at, carry):
            for p in range(PIECES):
                chain_copy(at, p).wait_send()
            return carry

        lax.fori_loop(0, z + 1, step, 0)

    def left_side(at, carry):
        for p in range(PIECES):
            side_copy(y, at, p).wait_send()
        return carry

    lax.fori_loop(0, z + 1 - y, left_side, 0)


def solution(mesh):
    cycle = mesh.shape["seq"]
    trajs = mesh.shape["group"]

    def per_device(pq, pk, pv, lengths, vq, vk, vv, owner, cached):
        tokens = pq.shape[1]
        rows = vq.shape[0] * vq.shape[1]
        width = HQ // cycle * HD
        slots = cycle * tokens
        bf16 = jnp.bfloat16
        vmem = pl.BlockSpec(memory_space=pltpu.VMEM)
        smem = pl.BlockSpec(memory_space=pltpu.SMEM)
        dma = pltpu.SemaphoreType.DMA
        chain = cycle // 2
        return pl.pallas_call(
            functools.partial(kernel, cycle, trajs),
            out_shape=(
                jax.ShapeDtypeStruct(pq.shape, bf16),
                jax.ShapeDtypeStruct(vq.shape, bf16),
            ),
            in_specs=[smem] * 3 + [vmem] * 6,
            out_specs=(vmem, vmem),
            scratch_shapes=[
                pltpu.VMEM((HK, slots, 2 * HD), bf16),
                pltpu.VMEM((trajs, slots, 2 * HD), bf16),
                pltpu.VMEM((cycle, rows, width + 2 * HD), bf16),
                pltpu.VMEM((cycle, rows, width + 2 * HD), bf16),
                pltpu.VMEM((cycle, rows, width), bf16),
                pltpu.VMEM((cycle, rows, width), bf16),
                pltpu.VMEM((tokens, slots), jnp.float32),
                dma((cycle,)), dma((cycle,)),
                dma((cycle,)), dma((cycle,)),
                dma((trajs, cycle)), dma((trajs, cycle)),
                dma((chain, PIECES)), dma((chain, PIECES)),
                dma((chain, PIECES)), dma((chain, PIECES)),
                dma((cycle,)), dma((cycle,)),
            ],
            compiler_params=pltpu.CompilerParams(
                collective_id=0, has_side_effects=True, vmem_limit_bytes=56 * 1024 * 1024
            ),
        )(lengths, owner, cached, pq, pk, pv, vq, vk, vv)

    in_specs = (
        P("group", "seq", None),
        P("group", "seq", None),
        P("group", "seq", None),
        P(),
        P(("group", "seq"), None, None),
        P(("group", "seq"), None, None),
        P(("group", "seq"), None, None),
        P(),
        P(),
    )
    out_specs = (P("group", "seq", None), P(("group", "seq"), None, None))
    return jax.shard_map(
        per_device, mesh=mesh, in_specs=in_specs, out_specs=out_specs, check_vma=False
    )
```

```python
import functools
import math

import jax
import jax.numpy as jnp
from jax import lax
from jax.experimental import pallas as pl
from jax.experimental.pallas import tpu as pltpu
from jax.sharding import PartitionSpec as P

HQ = 64
HK = 8
HD = 128
BLK = 64
PIECES = 4
VERIFY_SET = 4
LOW = -1e30
MESH = pl.DeviceIdType.MESH
FACTOR = HD ** (-0.5) * math.log2(math.e)


def dot_t(a, b):
    return lax.dot_general(a, b, (((1,), (1,)), ((), ())), preferred_element_type=jnp.float32)


def kernel(
    cycle, trajs, lengths, owner, cached, pq_hbm, pk, pv, vq, vk, vv, pout, vout,
    pq, obuf, kvbuf, cache, qsend, qland, osend, oland, bias,
    l_sem, q_send, q_recv, c_send, c_recv, g_send, g_recv, z_send, z_recv, y_send, y_recv, o_send, o_recv,
):
    g = lax.axis_index("group")
    s = lax.axis_index("seq")
    tokens = pq.shape[0]
    local_rows, steps = vq.shape[0], vq.shape[1]
    rows = local_rows * steps
    slots = cycle * tokens
    own_heads = HQ // cycle
    per_head = cycle // HK
    width = own_heads * HD
    row_count = local_rows * cycle
    group = HQ // HK
    chain = cycle // 2
    z = s // 2
    y = s % 2
    heads = HK // PIECES

    fetch = pltpu.make_async_copy(pq_hbm.at[0], pq, l_sem.at[PIECES])
    fetch.start()

    barrier = pltpu.get_barrier_semaphore()

    def greet(i, carry):
        pl.semaphore_signal(barrier, inc=1, device_id=(g, lax.rem(s + i, cycle)), device_id_type=MESH)
        return carry

    lax.fori_loop(1, cycle, greet, 0)
    for i in range(1, trajs):
        pl.semaphore_signal(barrier, inc=1, device_id=(lax.rem(g + i, trajs), s), device_id_type=MESH)

    def span(t):
        return pl.ds(pl.multiple_of(t * tokens, tokens), tokens)

    mine = span(s)
    for k in range(HK):
        kvbuf[k, mine, 0:HD] = pk[0, :, k * HD : (k + 1) * HD]
        kvbuf[k, mine, HD : 2 * HD] = pv[0, :, k * HD : (k + 1) * HD]
    wide_q = jnp.concatenate([vq[r].astype(jnp.float32) for r in range(local_rows)], axis=0)
    wide_k = jnp.concatenate([vk[r].astype(jnp.float32) for r in range(local_rows)], axis=0)
    wide_v = jnp.concatenate([vv[r].astype(jnp.float32) for r in range(local_rows)], axis=0)
    for t in range(cycle):
        k = t // per_head
        qsend[t, :, 0:width] = wide_q[:, t * width : (t + 1) * width].astype(jnp.bfloat16)
        qsend[t, :, width : width + HD] = wide_k[:, k * HD : (k + 1) * HD].astype(jnp.bfloat16)
        qsend[t, :, width + HD : width + 2 * HD] = wide_v[:, k * HD : (k + 1) * HD].astype(jnp.bfloat16)
    pl.semaphore_wait(barrier, cycle - 1 + trajs - 1)

    def row_copy(to, source):
        return pltpu.make_async_remote_copy(
            src_ref=qsend.at[to], dst_ref=qland.at[source],
            send_sem=q_send.at[to], recv_sem=q_recv.at[source],
            device_id=(g, to), device_id_type=MESH,
        )

    def head_copy(to, source):
        return pltpu.make_async_remote_copy(
            src_ref=kvbuf.at[to // per_head, span(source)], dst_ref=cache.at[g, span(source)],
            send_sem=c_send.at[to], recv_sem=c_recv.at[source],
            device_id=(g, to), device_id_type=MESH,
        )

    def group_copy(to, traj, t):
        return pltpu.make_async_remote_copy(
            src_ref=cache.at[traj, span(t)], dst_ref=cache.at[traj, span(t)],
            send_sem=g_send.at[to, t], recv_sem=g_recv.at[traj, t],
            device_id=(to, s), device_id_type=MESH,
        )

    def piece(line, at, p):
        return kvbuf.at[pl.ds(p * heads, heads), span(2 * at + line)]

    def chain_copy(at, p):
        return pltpu.make_async_remote_copy(
            src_ref=piece(y, at, p), dst_ref=piece(y, at, p),
            send_sem=z_send.at[at, p], recv_sem=z_recv.at[at, p],
            device_id=(g, lax.rem(s + 2, cycle)), device_id_type=MESH,
        )

    def side_copy(line, at, p):
        return pltpu.make_async_remote_copy(
            src_ref=piece(line, at, p), dst_ref=piece(line, at, p),
            send_sem=y_send.at[at, p], recv_sem=y_recv.at[at, p],
            device_id=(g, s + 1 - 2 * y), device_id_type=MESH,
        )

    def out_copy(to, source):
        return pltpu.make_async_remote_copy(
            src_ref=osend.at[to], dst_ref=oland.at[source],
            send_sem=o_send.at[to], recv_sem=o_recv.at[source],
            device_id=(g, to), device_id_type=MESH,
        )

    def send_first(i, carry):
        to = lax.rem(s + i, cycle)
        head_copy(to, s).start()
        return carry

    lax.fori_loop(1, cycle, send_first, 0)

    def send_rows(i, carry):
        to = lax.rem(s + i, cycle)
        row_copy(to, s).start()
        return carry

    lax.fori_loop(1, cycle, send_rows, 0)
    for p in range(PIECES):
        @pl.when(z < chain - 1)
        def _():
            chain_copy(z, p).start()

        @pl.when(y == 0)
        def _():
            side_copy(y, z, p).start()

    cache[g, mine, :] = kvbuf[s // per_head, mine, :]
    qland[s] = qsend[s]
    for i in range(1, trajs):
        group_copy(lax.rem(g + i, trajs), g, s).start()

    def blank(t, carry):
        kvbuf[:, span(t), :] = jnp.zeros((HK, tokens, 2 * HD), jnp.bfloat16)
        return carry

    lax.fori_loop(s + 1, cycle, blank, 0)
    length = lengths[g]
    column = lax.broadcasted_iota(jnp.int32, (tokens, slots), 1)
    slot = s * tokens + lax.broadcasted_iota(jnp.int32, (tokens, slots), 0)
    bias[...] = jnp.where((column <= slot) & (column < length), 0.0, LOW)

    def pass_heads(i, carry):
        t = lax.rem(s + i, cycle)
        head_copy(s, t).wait_recv()
        for j in range(1, trajs):
            group_copy(lax.rem(g + j, trajs), g, t).start()
        return carry

    lax.fori_loop(1, cycle, pass_heads, 0)

    def forward(d, p):
        @pl.when(d <= z)
        def _():
            at = z - d
            chain_copy(at, p).wait_recv()

            @pl.when(z < chain - 1)
            def _():
                chain_copy(at, p).start()

            side_copy(y, at, p).start()

    def forward_all(low, high):
        def step(d, carry):
            for p in range(PIECES):
                forward(d, p)
            return carry

        lax.fori_loop(low, high, step, 0)

    def verify_set(sources):
        count = own_heads * rows
        index = lax.broadcasted_iota(jnp.int32, (count, 1), 0) % rows
        row_of = index // steps
        where_to = lax.broadcasted_iota(jnp.int32, (count, slots), 1)
        fresh_col = lax.broadcasted_iota(jnp.int32, (count, rows), 1)
        allowed = (fresh_col // steps == row_of) & (fresh_col % steps <= index % steps)
        owners, both, weighed = [], [], []
        for t in sources:
            wide = qland[t].astype(jnp.float32)
            queries = jnp.concatenate(
                [wide[:, h * HD : (h + 1) * HD] for h in range(own_heads)], axis=0
            ).astype(jnp.bfloat16)
            scores, limits, whos = None, None, []
            for r in range(local_rows):
                row = g * row_count + t * local_rows + r
                who = owner[row]
                whos.append(who)
                limit = jnp.minimum(cached[row] * BLK, lengths[who])
                part = dot_t(queries, cache[who, :, 0:HD])
                scores = part if r == 0 else jnp.where(row_of == r, part, scores)
                limits = jnp.full((count, 1), limit) if r == 0 else jnp.where(row_of == r, limit, limits)
            owners.append(whos)
            fresh = dot_t(queries, qland[t, :, width : width + HD])
            both.append((jnp.where(where_to < limits, scores, LOW), jnp.where(allowed, fresh, LOW)))
        for scores, fresh in both:
            highest = jnp.maximum(
                jnp.max(scores, axis=-1, keepdims=True), jnp.max(fresh, axis=-1, keepdims=True)
            )
            weights = jnp.exp2((scores - highest) * FACTOR)
            fresh_weights = jnp.exp2((fresh - highest) * FACTOR)
            total = jnp.sum(weights, axis=-1, keepdims=True)
            total = total + jnp.sum(fresh_weights, axis=-1, keepdims=True)
            weighed.append((weights, fresh_weights.astype(jnp.bfloat16), total))
        results = []
        for t, whos, (weights, fresh_weights, total) in zip(sources, owners, weighed):
            mixed = jnp.dot(
                fresh_weights,
                qland[t, :, width + HD : width + 2 * HD],
                preferred_element_type=jnp.float32,
            )
            for r in range(local_rows):
                chosen = jnp.where(row_of == r, weights, 0.0).astype(jnp.bfloat16)
                mixed = mixed + jnp.dot(
                    chosen, cache[whos[r], :, HD : 2 * HD], preferred_element_type=jnp.float32
                )
            results.append((mixed / total).astype(jnp.bfloat16))
        for t, result in zip(sources, results):
            for h in range(own_heads):
                osend[t, :, h * HD : (h + 1) * HD] = result[h * rows : (h + 1) * rows]

    def verify_some(low, high):
        def step(i, carry):
            first = low + i * VERIFY_SET
            verify_set([lax.rem(s + first + j, cycle) for j in range(VERIFY_SET)])
            for j in range(VERIFY_SET):
                @pl.when(first + j < cycle)
                def _():
                    out_copy(lax.rem(s + first + j, cycle), s).start()

            return carry

        lax.fori_loop(0, (high - low) // VERIFY_SET, step, 0)

    tile = max(1, min(group, (512 * 512) // (tokens * slots)))

    def attend(k, part):
        first = k * group + part * tile
        queries = jnp.concatenate(
            [pq[:, pl.ds(pl.multiple_of((first + h) * HD, HD), HD)] for h in range(tile)], axis=0
        )
        scores = dot_t(queries, kvbuf[k, :, 0:HD]).reshape(tile, tokens, slots) + bias[...][None]
        highest = jnp.max(scores, axis=-1, keepdims=True)
        weights = jnp.exp2((scores - highest) * FACTOR)
        total = jnp.sum(weights, axis=-1, keepdims=True)
        mixed = jnp.dot(
            weights.astype(jnp.bfloat16).reshape(tile * tokens, slots),
            kvbuf[k, :, HD : 2 * HD],
            preferred_element_type=jnp.float32,
        )
        result = (mixed / total.reshape(tile * tokens, 1)).astype(jnp.bfloat16)
        for h in range(tile):
            obuf[:, pl.ds(pl.multiple_of((first + h) * HD, HD), HD)] = result[
                h * tokens : (h + 1) * tokens
            ]

    def prefill_piece(p):
        def wait_one(at, carry):
            side_copy(1 - y, at, p).wait_recv()
            return carry

        lax.fori_loop(0, z + y, wait_one, 0)

        parts = group // tile
        total = heads * parts
        unroll = heads if parts == 1 else 1

        def step(i, carry):
            for j in range(unroll):
                at = i * unroll + j
                attend(p * heads + at // parts, at % parts)
            return carry

        lax.fori_loop(0, total // unroll, step, 0)
        piece_out(p).start()

    def piece_out(p):
        lanes = pl.ds(p * heads * group * HD, heads * group * HD)
        return pltpu.make_async_copy(obuf.at[:, lanes], pout.at[0, :, lanes], l_sem.at[p])

    forward_all(1, chain - 2)

    def rows_arrive(i, carry):
        row_copy(s, lax.rem(s + i, cycle)).wait_recv()
        return carry

    lax.fori_loop(1, cycle, rows_arrive, 0)

    def caches_arrive(t, carry):
        for i in range(1, trajs):
            group_copy(g, lax.rem(g + i, trajs), t).wait_recv()
        return carry

    lax.fori_loop(0, cycle, caches_arrive, 0)
    verify_some(1, cycle // 2 + 1)
    forward_all(chain - 2, chain - 1)
    verify_some(cycle // 2 + 1, cycle + 1)
    oland[s] = osend[s]
    fetch.wait()
    forward(chain - 1, 0)
    for p in range(PIECES):
        if p + 1 < PIECES:
            forward(chain - 1, p + 1)
        prefill_piece(p)

    def outs_arrive(i, carry):
        out_copy(s, lax.rem(s + i, cycle)).wait_recv()
        return carry

    lax.fori_loop(1, cycle, outs_arrive, 0)
    for t in range(cycle):
        block = oland[t].astype(jnp.float32)
        for r in range(local_rows):
            vout[r, :, t * width : (t + 1) * width] = block[r * steps : (r + 1) * steps].astype(
                jnp.bfloat16
            )

    for p in range(PIECES):
        piece_out(p).wait()

    def left(i, carry):
        to = lax.rem(s + i, cycle)
        head_copy(to, s).wait_send()
        row_copy(to, s).wait_send()
        out_copy(to, s).wait_send()
        return carry

    lax.fori_loop(1, cycle, left, 0)

    def left_group(t, carry):
        for i in range(1, trajs):
            group_copy(lax.rem(g + i, trajs), g, t).wait_send()
        return carry

    lax.fori_loop(0, cycle, left_group, 0)

    @pl.when(z < chain - 1)
    def _():
        def step(at, carry):
            for p in range(PIECES):
                chain_copy(at, p).wait_send()
            return carry

        lax.fori_loop(0, z + 1, step, 0)

    def left_side(at, carry):
        for p in range(PIECES):
            side_copy(y, at, p).wait_send()
        return carry

    lax.fori_loop(0, z + 1 - y, left_side, 0)


def hand_on(a, b, a_out, b_out, sems):
    count = 4 if a.shape[1] % 64 == 0 else 1
    size = a.shape[1] // count
    copies = [
        pltpu.make_async_copy(
            a.at[:, pl.ds(i * size, size)], a_out.at[:, pl.ds(i * size, size)], sems.at[i]
        )
        for i in range(count)
    ]
    copies.append(pltpu.make_async_copy(b, b_out, sems.at[4]))
    for copy in copies:
        copy.start()
    for copy in copies:
        copy.wait()


def solution(mesh):
    cycle = mesh.shape["seq"]
    trajs = mesh.shape["group"]

    def per_device(pq, pk, pv, lengths, vq, vk, vv, owner, cached):
        tokens = pq.shape[1]
        rows = vq.shape[0] * vq.shape[1]
        width = HQ // cycle * HD
        slots = cycle * tokens
        bf16 = jnp.bfloat16
        vmem = pl.BlockSpec(memory_space=pltpu.VMEM)
        anywhere = pl.BlockSpec(memory_space=pl.ANY)
        smem = pl.BlockSpec(memory_space=pltpu.SMEM)
        dma = pltpu.SemaphoreType.DMA
        chain = cycle // 2
        outs = pl.pallas_call(
            functools.partial(kernel, cycle, trajs),
            out_shape=(
                jax.ShapeDtypeStruct(pq.shape, bf16),
                jax.ShapeDtypeStruct(vq.shape, bf16),
            ),
            in_specs=[smem] * 3 + [anywhere] + [vmem] * 5,
            out_specs=(anywhere, vmem),
            scratch_shapes=[
                pltpu.VMEM(pq.shape[1:], bf16),
                pltpu.VMEM(pq.shape[1:], bf16),
                pltpu.VMEM((HK, slots, 2 * HD), bf16),
                pltpu.VMEM((trajs, slots, 2 * HD), bf16),
                pltpu.VMEM((cycle, rows, width + 2 * HD), bf16),
                pltpu.VMEM((cycle, rows, width + 2 * HD), bf16),
                pltpu.VMEM((cycle, rows, width), bf16),
                pltpu.VMEM((cycle, rows, width), bf16),
                pltpu.VMEM((tokens, slots), jnp.float32),
                dma((PIECES + 1,)),
                dma((cycle,)), dma((cycle,)),
                dma((cycle,)), dma((cycle,)),
                dma((trajs, cycle)), dma((trajs, cycle)),
                dma((chain, PIECES)), dma((chain, PIECES)),
                dma((chain, PIECES)), dma((chain, PIECES)),
                dma((cycle,)), dma((cycle,)),
            ],
            compiler_params=pltpu.CompilerParams(
                collective_id=0, has_side_effects=True, vmem_limit_bytes=56 * 1024 * 1024
            ),
        )(lengths, owner, cached, pq, pk, pv, vq, vk, vv)
        return pl.pallas_call(
            hand_on,
            out_shape=(
                jax.ShapeDtypeStruct(pq.shape, bf16),
                jax.ShapeDtypeStruct(vq.shape, bf16),
            ),
            in_specs=[anywhere] * 2,
            out_specs=(anywhere, anywhere),
            scratch_shapes=[dma((5,))],
            compiler_params=pltpu.CompilerParams(vmem_limit_bytes=60 * 1024 * 1024),
        )(*outs)

    in_specs = (
        P("group", "seq", None),
        P("group", "seq", None),
        P("group", "seq", None),
        P(),
        P(("group", "seq"), None, None),
        P(("group", "seq"), None, None),
        P(("group", "seq"), None, None),
        P(),
        P(),
    )
    out_specs = (P("group", "seq", None), P(("group", "seq"), None, None))
    return jax.shard_map(
        per_device, mesh=mesh, in_specs=in_specs, out_specs=out_specs, check_vma=False
    )
```

```python
import functools
import math

import jax
import jax.numpy as jnp
from jax import lax
from jax.experimental import pallas as pl
from jax.experimental.pallas import tpu as pltpu
from jax.sharding import PartitionSpec as P

HQ = 64
HK = 8
HD = 128
BLK = 64
PIECES = 4
VERIFY_SET = 4
HAND = 4
LOW = -1e30
MESH = pl.DeviceIdType.MESH
FACTOR = HD ** (-0.5) * math.log2(math.e)


def dot_t(a, b):
    return lax.dot_general(a, b, (((1,), (1,)), ((), ())), preferred_element_type=jnp.float32)


def kernel(
    cycle, trajs, lengths, owner, cached, pq_hbm, pk, pv, vq, vk, vv, pout, vout,
    pq, obuf, kvbuf, cache, qsend, qland, osend, oland, bias,
    l_sem, q_send, q_recv, c_send, c_recv, g_send, g_recv, z_send, z_recv, y_send, y_recv, o_send, o_recv,
):
    g = lax.axis_index("group")
    s = lax.axis_index("seq")
    tokens = pq.shape[0]
    local_rows, steps = vq.shape[0], vq.shape[1]
    rows = local_rows * steps
    slots = cycle * tokens
    own_heads = HQ // cycle
    per_head = cycle // HK
    width = own_heads * HD
    row_count = local_rows * cycle
    pair = g // 2 * 2
    core = g % 2
    low = cycle // 2
    sources = 2 * cycle
    me = core * cycle + s
    unit = 2 * s + core
    group = HQ // HK
    chain = cycle // 2
    z = s // 2
    y = s % 2
    heads = HK // PIECES

    fetch = pltpu.make_async_copy(pq_hbm.at[0], pq, l_sem.at[PIECES])
    fetch.start()

    barrier = pltpu.get_barrier_semaphore()

    def greet(i, carry):
        other = lax.rem(me + i, sources)
        pl.semaphore_signal(
            barrier, inc=1, device_id=(pair + other // cycle, other % cycle), device_id_type=MESH
        )
        return carry

    lax.fori_loop(1, sources, greet, 0)
    for i in range(1, trajs // 2):
        pl.semaphore_signal(
            barrier, inc=1, device_id=(lax.rem(g + 2 * i, trajs), s), device_id_type=MESH
        )

    def span(t):
        return pl.ds(pl.multiple_of(t * tokens, tokens), tokens)

    mine = span(s)
    for k in range(HK):
        kvbuf[k, mine, 0:HD] = pk[0, :, k * HD : (k + 1) * HD]
        kvbuf[k, mine, HD : 2 * HD] = pv[0, :, k * HD : (k + 1) * HD]
    wide_q = jnp.concatenate([vq[r].astype(jnp.float32) for r in range(local_rows)], axis=0)
    wide_k = jnp.concatenate([vk[r].astype(jnp.float32) for r in range(local_rows)], axis=0)
    wide_v = jnp.concatenate([vv[r].astype(jnp.float32) for r in range(local_rows)], axis=0)
    for t in range(cycle):
        k = t // per_head
        qsend[t, :, 0:width] = wide_q[:, t * width : (t + 1) * width].astype(jnp.bfloat16)
        qsend[t, :, width : width + HD] = wide_k[:, k * HD : (k + 1) * HD].astype(jnp.bfloat16)
        qsend[t, :, width + HD : width + 2 * HD] = wide_v[:, k * HD : (k + 1) * HD].astype(jnp.bfloat16)
    pl.semaphore_wait(barrier, sources - 1 + trajs // 2 - 1)

    def row_copy(u, source):
        return pltpu.make_async_remote_copy(
            src_ref=qsend.at[u], dst_ref=qland.at[source],
            send_sem=q_send.at[u], recv_sem=q_recv.at[source],
            device_id=(pair + u % 2, u // 2), device_id_type=MESH,
        )

    def head_copy(u, source):
        at = (pair + source // cycle, span(source % cycle))
        return pltpu.make_async_remote_copy(
            src_ref=kvbuf.at[u // per_head, span(source % cycle)], dst_ref=cache.at[at[0], at[1]],
            send_sem=c_send.at[u], recv_sem=c_recv.at[source],
            device_id=(pair + u % 2, u // 2), device_id_type=MESH,
        )

    def group_copy(step, traj, t):
        return pltpu.make_async_remote_copy(
            src_ref=cache.at[traj, span(t)], dst_ref=cache.at[traj, span(t)],
            send_sem=g_send.at[step, traj, t], recv_sem=g_recv.at[traj, t],
            device_id=(lax.rem(g + 2 * step, trajs), s), device_id_type=MESH,
        )

    def piece(line, at, p):
        return kvbuf.at[pl.ds(p * heads, heads), span(2 * at + line)]

    def chain_copy(at, p):
        return pltpu.make_async_remote_copy(
            src_ref=piece(y, at, p), dst_ref=piece(y, at, p),
            send_sem=z_send.at[at, p], recv_sem=z_recv.at[at, p],
            device_id=(g, lax.rem(s + 2, cycle)), device_id_type=MESH,
        )

    def side_copy(line, at, p):
        return pltpu.make_async_remote_copy(
            src_ref=piece(line, at, p), dst_ref=piece(line, at, p),
            send_sem=y_send.at[at, p], recv_sem=y_recv.at[at, p],
            device_id=(g, s + 1 - 2 * y), device_id_type=MESH,
        )

    def out_copy(to, source):
        return pltpu.make_async_remote_copy(
            src_ref=osend.at[to], dst_ref=oland.at[source],
            send_sem=o_send.at[to], recv_sem=o_recv.at[source],
            device_id=(pair + to // cycle, to % cycle), device_id_type=MESH,
        )

    def to_units(act):
        def step(u, carry):
            @pl.when(u != unit)
            def _():
                act(u)

            return carry

        lax.fori_loop(0, cycle, step, 0)

    for p in range(PIECES):
        @pl.when(z < chain - 1)
        def _():
            chain_copy(z, p).start()

    to_units(lambda u: head_copy(u, me).start())
    for p in range(PIECES):
        @pl.when(y == 0)
        def _():
            side_copy(y, z, p).start()

    to_units(lambda u: row_copy(u, me).start())

    @pl.when(s < low)
    def _():
        cache[g, mine, :] = kvbuf[unit // per_head, mine, :]
        qland[me] = qsend[unit]
        for i in range(1, trajs // 2):
            group_copy(i, g, s).start()

    def blank(t, carry):
        kvbuf[:, span(t), :] = jnp.zeros((HK, tokens, 2 * HD), jnp.bfloat16)
        return carry

    lax.fori_loop(s + 1, cycle, blank, 0)
    length = lengths[g]
    column = lax.broadcasted_iota(jnp.int32, (tokens, slots), 1)
    slot = s * tokens + lax.broadcasted_iota(jnp.int32, (tokens, slots), 0)
    bias[...] = jnp.where((column <= slot) & (column < length), 0.0, LOW)

    def pass_heads(i, carry):
        source = lax.rem(me + i, sources)
        head_copy(unit, source).wait_recv()
        for j in range(1, trajs // 2):
            group_copy(j, pair + source // cycle, source % cycle).start()
        return carry

    def forward(d, p):
        @pl.when(d <= z)
        def _():
            at = z - d
            chain_copy(at, p).wait_recv()

            @pl.when(z < chain - 1)
            def _():
                chain_copy(at, p).start()

            side_copy(y, at, p).start()

    def forward_all(low, high):
        def step(d, carry):
            for p in range(PIECES):
                forward(d, p)
            return carry

        lax.fori_loop(low, high, step, 0)

    def verify_set(chosen_sources):
        count = own_heads * rows
        index = lax.broadcasted_iota(jnp.int32, (count, 1), 0) % rows
        row_of = index // steps
        where_to = lax.broadcasted_iota(jnp.int32, (count, slots), 1)
        fresh_col = lax.broadcasted_iota(jnp.int32, (count, rows), 1)
        allowed = (fresh_col // steps == row_of) & (fresh_col % steps <= index % steps)
        owners, both, weighed = [], [], []
        for t in chosen_sources:
            wide = qland[t].astype(jnp.float32)
            queries = jnp.concatenate(
                [wide[:, h * HD : (h + 1) * HD] for h in range(own_heads)], axis=0
            ).astype(jnp.bfloat16)
            scores, limits, whos = None, None, []
            for r in range(local_rows):
                row = (pair + t // cycle) * row_count + (t % cycle) * local_rows + r
                who = owner[row]
                whos.append(who)
                limit = jnp.minimum(cached[row] * BLK, lengths[who])
                part = dot_t(queries, cache[who, :, 0:HD])
                scores = part if r == 0 else jnp.where(row_of == r, part, scores)
                limits = jnp.full((count, 1), limit) if r == 0 else jnp.where(row_of == r, limit, limits)
            owners.append(whos)
            fresh = dot_t(queries, qland[t, :, width : width + HD])
            both.append((jnp.where(where_to < limits, scores, LOW), jnp.where(allowed, fresh, LOW)))
        for scores, fresh in both:
            highest = jnp.maximum(
                jnp.max(scores, axis=-1, keepdims=True), jnp.max(fresh, axis=-1, keepdims=True)
            )
            weights = jnp.exp2((scores - highest) * FACTOR)
            fresh_weights = jnp.exp2((fresh - highest) * FACTOR)
            total = jnp.sum(weights, axis=-1, keepdims=True)
            total = total + jnp.sum(fresh_weights, axis=-1, keepdims=True)
            weighed.append((weights, fresh_weights.astype(jnp.bfloat16), total))
        results = []
        for t, whos, (weights, fresh_weights, total) in zip(chosen_sources, owners, weighed):
            mixed = jnp.dot(
                fresh_weights,
                qland[t, :, width + HD : width + 2 * HD],
                preferred_element_type=jnp.float32,
            )
            for r in range(local_rows):
                chosen = jnp.where(row_of == r, weights, 0.0).astype(jnp.bfloat16)
                mixed = mixed + jnp.dot(
                    chosen, cache[whos[r], :, HD : 2 * HD], preferred_element_type=jnp.float32
                )
            results.append((mixed / total).astype(jnp.bfloat16))
        for t, result in zip(chosen_sources, results):
            for h in range(own_heads):
                osend[t, :, h * HD : (h + 1) * HD] = result[h * rows : (h + 1) * rows]

    def verify_all():
        def step(i, carry):
            first = 1 + i * VERIFY_SET
            verify_set([lax.rem(me + first + j, sources) for j in range(VERIFY_SET)])
            for j in range(VERIFY_SET):
                @pl.when(first + j < sources)
                def _():
                    out_copy(lax.rem(me + first + j, sources), unit).start()

            return carry

        lax.fori_loop(0, sources // VERIFY_SET, step, 0)
        oland[unit] = osend[me]

    tile = max(1, min(group, (512 * 512) // (tokens * slots)))

    def attend(k, part, seen):
        first = k * group + part * tile
        queries = jnp.concatenate(
            [pq[:, pl.ds(pl.multiple_of((first + h) * HD, HD), HD)] for h in range(tile)], axis=0
        )
        scores = dot_t(queries, kvbuf[k, 0:seen, 0:HD]).reshape(tile, tokens, seen) + bias[:, 0:seen][None]
        highest = jnp.max(scores, axis=-1, keepdims=True)
        weights = jnp.exp2((scores - highest) * FACTOR)
        total = jnp.sum(weights, axis=-1, keepdims=True)
        mixed = jnp.dot(
            weights.astype(jnp.bfloat16).reshape(tile * tokens, seen),
            kvbuf[k, 0:seen, HD : 2 * HD],
            preferred_element_type=jnp.float32,
        )
        result = (mixed / total.reshape(tile * tokens, 1)).astype(jnp.bfloat16)
        for h in range(tile):
            obuf[:, pl.ds(pl.multiple_of((first + h) * HD, HD), HD)] = result[
                h * tokens : (h + 1) * tokens
            ]

    def prefill_piece(p):
        def wait_one(at, carry):
            side_copy(1 - y, at, p).wait_recv()
            return carry

        lax.fori_loop(0, z + y, wait_one, 0)

        parts = group // tile
        total = heads * parts
        unroll = heads if parts == 1 else 1

        def sweep(seen):
            def step(i, carry):
                for j in range(unroll):
                    at = i * unroll + j
                    attend(p * heads + at // parts, at % parts, seen)
                return carry

            lax.fori_loop(0, total // unroll, step, 0)

        @pl.when(s < low)
        def _():
            sweep(low * tokens)

        @pl.when(s >= low)
        def _():
            sweep(slots)

        piece_out(p).start()

    def piece_out(p):
        lanes = pl.ds(p * heads * group * HD, heads * group * HD)
        return pltpu.make_async_copy(obuf.at[:, lanes], pout.at[0, :, lanes], l_sem.at[p])

    forward_all(1, 2)

    @pl.when(s < low)
    def _():
        lax.fori_loop(1, sources, pass_heads, 0)

    forward_all(2, chain - 1)
    fetch.wait()
    forward(chain - 1, 0)
    for p in range(PIECES):
        if p + 1 < PIECES:
            forward(chain - 1, p + 1)
        prefill_piece(p)

    @pl.when(s < low)
    def _():
        def rows_arrive(i, carry):
            row_copy(unit, lax.rem(me + i, sources)).wait_recv()
            return carry

        lax.fori_loop(1, sources, rows_arrive, 0)

        def caches_arrive(t, carry):
            for i in range(2, trajs):
                group_copy(1, lax.rem(pair + i, trajs), t).wait_recv()
            return carry

        lax.fori_loop(0, cycle, caches_arrive, 0)
        verify_all()

    to_units(lambda u: out_copy(me, u).wait_recv())
    for t in range(cycle):
        block = oland[t].astype(jnp.float32)
        for r in range(local_rows):
            vout[r, :, t * width : (t + 1) * width] = block[r * steps : (r + 1) * steps].astype(
                jnp.bfloat16
            )

    for p in range(PIECES):
        piece_out(p).wait()

    to_units(lambda u: head_copy(u, me).wait_send())
    to_units(lambda u: row_copy(u, me).wait_send())

    @pl.when(s < low)
    def _():
        def left(i, carry):
            out_copy(lax.rem(me + i, sources), unit).wait_send()
            return carry

        lax.fori_loop(1, sources, left, 0)

        def left_group(t, carry):
            for j in range(1, trajs // 2):
                for c in range(2):
                    group_copy(j, pair + c, t).wait_send()
            return carry

        lax.fori_loop(0, cycle, left_group, 0)

    @pl.when(z < chain - 1)
    def _():
        def step(at, carry):
            for p in range(PIECES):
                chain_copy(at, p).wait_send()
            return carry

        lax.fori_loop(0, z + 1, step, 0)

    def left_side(at, carry):
        for p in range(PIECES):
            side_copy(y, at, p).wait_send()
        return carry

    lax.fori_loop(0, z + 1 - y, left_side, 0)


def hand_on(count, a, b, a_out, b_out, held, held_b, sems):
    size = a.shape[1] // count
    arrive = [
        pltpu.make_async_copy(
            a.at[:, pl.ds(i * size, size)], held.at[:, pl.ds(i * size, size)], sems.at[i]
        )
        for i in range(count)
    ]
    leave = [
        pltpu.make_async_copy(
            held.at[:, pl.ds(i * size, size)], a_out.at[:, pl.ds(i * size, size)], sems.at[i]
        )
        for i in range(count)
    ]
    arrive.append(pltpu.make_async_copy(b, held_b, sems.at[count]))
    leave.append(pltpu.make_async_copy(held_b, b_out, sems.at[count]))
    for copy in arrive:
        copy.start()
    for here, there in zip(arrive, leave):
        here.wait()
        there.start()
    for copy in leave:
        copy.wait()


def solution(mesh):
    cycle = mesh.shape["seq"]
    trajs = mesh.shape["group"]

    def per_device(pq, pk, pv, lengths, vq, vk, vv, owner, cached):
        tokens = pq.shape[1]
        rows = vq.shape[0] * vq.shape[1]
        width = HQ // cycle * HD
        slots = cycle * tokens
        bf16 = jnp.bfloat16
        vmem = pl.BlockSpec(memory_space=pltpu.VMEM)
        anywhere = pl.BlockSpec(memory_space=pl.ANY)
        smem = pl.BlockSpec(memory_space=pltpu.SMEM)
        dma = pltpu.SemaphoreType.DMA
        chain = cycle // 2
        outs = pl.pallas_call(
            functools.partial(kernel, cycle, trajs),
            out_shape=(
                jax.ShapeDtypeStruct(pq.shape, bf16),
                jax.ShapeDtypeStruct(vq.shape, bf16),
            ),
            in_specs=[smem] * 3 + [anywhere] + [vmem] * 5,
            out_specs=(anywhere, vmem),
            scratch_shapes=[
                pltpu.VMEM(pq.shape[1:], bf16),
                pltpu.VMEM(pq.shape[1:], bf16),
                pltpu.VMEM((HK, slots, 2 * HD), bf16),
                pltpu.VMEM((trajs, slots, 2 * HD), bf16),
                pltpu.VMEM((cycle, rows, width + 2 * HD), bf16),
                pltpu.VMEM((2 * cycle, rows, width + 2 * HD), bf16),
                pltpu.VMEM((2 * cycle, rows, width), bf16),
                pltpu.VMEM((cycle, rows, width), bf16),
                pltpu.VMEM((tokens, slots), jnp.float32),
                dma((PIECES + 1,)),
                dma((cycle,)), dma((2 * cycle,)),
                dma((cycle,)), dma((2 * cycle,)),
                dma((trajs // 2, trajs, cycle)), dma((trajs, cycle)),
                dma((chain, PIECES)), dma((chain, PIECES)),
                dma((chain, PIECES)), dma((chain, PIECES)),
                dma((2 * cycle,)), dma((cycle,)),
            ],
            compiler_params=pltpu.CompilerParams(
                collective_id=0, has_side_effects=True, vmem_limit_bytes=56 * 1024 * 1024
            ),
        )(lengths, owner, cached, pq, pk, pv, vq, vk, vv)
        return pl.pallas_call(
            functools.partial(hand_on, HAND),
            out_shape=(
                jax.ShapeDtypeStruct(pq.shape, bf16),
                jax.ShapeDtypeStruct(vq.shape, bf16),
            ),
            in_specs=[anywhere] * 2,
            out_specs=(anywhere, anywhere),
            scratch_shapes=[pltpu.VMEM(pq.shape, bf16), pltpu.VMEM(vq.shape, bf16), dma((HAND + 1,))],
            compiler_params=pltpu.CompilerParams(vmem_limit_bytes=60 * 1024 * 1024),
        )(*outs)

    in_specs = (
        P("group", "seq", None),
        P("group", "seq", None),
        P("group", "seq", None),
        P(),
        P(("group", "seq"), None, None),
        P(("group", "seq"), None, None),
        P(("group", "seq"), None, None),
        P(),
        P(),
    )
    out_specs = (P("group", "seq", None), P(("group", "seq"), None, None))
    return jax.shard_map(
        per_device, mesh=mesh, in_specs=in_specs, out_specs=out_specs, check_vma=False
    )
```

```python
import functools
import math

import jax
import jax.numpy as jnp
from jax import lax
from jax.experimental import pallas as pl
from jax.experimental.pallas import tpu as pltpu
from jax.sharding import PartitionSpec as P

HQ = 64
HK = 8
HD = 128
BLK = 64
PIECES = 4
VERIFY_SET = 4
HAND = 4
LOW = -1e30
MESH = pl.DeviceIdType.MESH
FACTOR = HD ** (-0.5) * math.log2(math.e)


def dot_t(a, b):
    return lax.dot_general(a, b, (((1,), (1,)), ((), ())), preferred_element_type=jnp.float32)


def kernel(
    cycle, trajs, lengths, owner, cached, pq_hbm, pk, pv, vq, vk, vv, pout, vout,
    pq, obuf, kvbuf, cache, qsend, qland, osend, oland, bias,
    l_sem, q_send, q_recv, c_send, c_recv, g_send, g_recv, z_send, z_recv, y_send, y_recv, o_send, o_recv,
):
    g = lax.axis_index("group")
    s = lax.axis_index("seq")
    tokens = pq.shape[0]
    local_rows, steps = vq.shape[0], vq.shape[1]
    rows = local_rows * steps
    slots = cycle * tokens
    own_heads = HQ // cycle
    per_head = cycle // HK
    width = own_heads * HD
    row_count = local_rows * cycle
    group = HQ // HK
    chain = cycle // 2
    z = s // 2
    y = s % 2
    heads = HK // PIECES

    fetch = pltpu.make_async_copy(pq_hbm.at[0], pq, l_sem.at[PIECES])
    fetch.start()

    barrier = pltpu.get_barrier_semaphore()

    def greet(i, carry):
        pl.semaphore_signal(barrier, inc=1, device_id=(g, lax.rem(s + i, cycle)), device_id_type=MESH)
        return carry

    lax.fori_loop(1, cycle, greet, 0)
    for i in range(1, trajs):
        pl.semaphore_signal(barrier, inc=1, device_id=(lax.rem(g + i, trajs), s), device_id_type=MESH)

    def span(t):
        return pl.ds(pl.multiple_of(t * tokens, tokens), tokens)

    mine = span(s)
    for k in range(HK):
        kvbuf[k, mine, 0:HD] = pk[0, :, k * HD : (k + 1) * HD]
        kvbuf[k, mine, HD : 2 * HD] = pv[0, :, k * HD : (k + 1) * HD]
    wide_q = jnp.concatenate([vq[r].astype(jnp.float32) for r in range(local_rows)], axis=0)
    wide_k = jnp.concatenate([vk[r].astype(jnp.float32) for r in range(local_rows)], axis=0)
    wide_v = jnp.concatenate([vv[r].astype(jnp.float32) for r in range(local_rows)], axis=0)
    for t in range(cycle):
        k = t // per_head
        qsend[t, :, 0:width] = wide_q[:, t * width : (t + 1) * width].astype(jnp.bfloat16)
        qsend[t, :, width : width + HD] = wide_k[:, k * HD : (k + 1) * HD].astype(jnp.bfloat16)
        qsend[t, :, width + HD : width + 2 * HD] = wide_v[:, k * HD : (k + 1) * HD].astype(jnp.bfloat16)
    pl.semaphore_wait(barrier, cycle - 1 + trajs - 1)

    def row_copy(to, source):
        return pltpu.make_async_remote_copy(
            src_ref=qsend.at[to], dst_ref=qland.at[source],
            send_sem=q_send.at[to], recv_sem=q_recv.at[source],
            device_id=(g, to), device_id_type=MESH,
        )

    def head_copy(to, source):
        return pltpu.make_async_remote_copy(
            src_ref=kvbuf.at[to // per_head, span(source)], dst_ref=cache.at[g, span(source)],
            send_sem=c_send.at[to], recv_sem=c_recv.at[source],
            device_id=(g, to), device_id_type=MESH,
        )

    def group_copy(to, traj, t):
        return pltpu.make_async_remote_copy(
            src_ref=cache.at[traj, span(t)], dst_ref=cache.at[traj, span(t)],
            send_sem=g_send.at[to, t], recv_sem=g_recv.at[traj, t],
            device_id=(to, s), device_id_type=MESH,
        )

    def piece(line, at, p):
        return kvbuf.at[pl.ds(p * heads, heads), span(2 * at + line)]

    def chain_copy(at, p):
        return pltpu.make_async_remote_copy(
            src_ref=piece(y, at, p), dst_ref=piece(y, at, p),
            send_sem=z_send.at[at, p], recv_sem=z_recv.at[at, p],
            device_id=(g, lax.rem(s + 2, cycle)), device_id_type=MESH,
        )

    def side_copy(line, at, p):
        return pltpu.make_async_remote_copy(
            src_ref=piece(line, at, p), dst_ref=piece(line, at, p),
            send_sem=y_send.at[at, p], recv_sem=y_recv.at[at, p],
            device_id=(g, s + 1 - 2 * y), device_id_type=MESH,
        )

    def out_copy(to, source):
        return pltpu.make_async_remote_copy(
            src_ref=osend.at[to], dst_ref=oland.at[source],
            send_sem=o_send.at[to], recv_sem=o_recv.at[source],
            device_id=(g, to), device_id_type=MESH,
        )

    def send_first(i, carry):
        to = lax.rem(s + i, cycle)
        head_copy(to, s).start()
        return carry

    lax.fori_loop(1, cycle, send_first, 0)

    def send_rows(i, carry):
        to = lax.rem(s + i, cycle)
        row_copy(to, s).start()
        return carry

    lax.fori_loop(1, cycle, send_rows, 0)
    for p in range(PIECES):
        @pl.when(z < chain - 1)
        def _():
            chain_copy(z, p).start()

        @pl.when(y == 0)
        def _():
            side_copy(y, z, p).start()

    cache[g, mine, :] = kvbuf[s // per_head, mine, :]
    qland[s] = qsend[s]
    for i in range(1, trajs):
        group_copy(lax.rem(g + i, trajs), g, s).start()

    def blank(t, carry):
        kvbuf[:, span(t), :] = jnp.zeros((HK, tokens, 2 * HD), jnp.bfloat16)
        return carry

    lax.fori_loop(s + 1, cycle, blank, 0)
    length = lengths[g]
    column = lax.broadcasted_iota(jnp.int32, (tokens, slots), 1)
    slot = s * tokens + lax.broadcasted_iota(jnp.int32, (tokens, slots), 0)
    bias[...] = jnp.where((column <= slot) & (column < length), 0.0, LOW)

    def pass_heads(i, carry):
        t = lax.rem(s + i, cycle)
        head_copy(s, t).wait_recv()
        for j in range(1, trajs):
            group_copy(lax.rem(g + j, trajs), g, t).start()
        return carry

    lax.fori_loop(1, cycle, pass_heads, 0)

    def forward(d, p):
        @pl.when(d <= z)
        def _():
            at = z - d
            chain_copy(at, p).wait_recv()

            @pl.when(z < chain - 1)
            def _():
                chain_copy(at, p).start()

            side_copy(y, at, p).start()

    def forward_all(low, high):
        def step(d, carry):
            for p in range(PIECES):
                forward(d, p)
            return carry

        lax.fori_loop(low, high, step, 0)

    def verify_set(sources):
        count = own_heads * rows
        index = lax.broadcasted_iota(jnp.int32, (count, 1), 0) % rows
        row_of = index // steps
        where_to = lax.broadcasted_iota(jnp.int32, (count, slots), 1)
        fresh_col = lax.broadcasted_iota(jnp.int32, (count, rows), 1)
        allowed = (fresh_col // steps == row_of) & (fresh_col % steps <= index % steps)
        owners, both, weighed = [], [], []
        for t in sources:
            wide = qland[t].astype(jnp.float32)
            queries = jnp.concatenate(
                [wide[:, h * HD : (h + 1) * HD] for h in range(own_heads)], axis=0
            ).astype(jnp.bfloat16)
            scores, limits, whos = None, None, []
            for r in range(local_rows):
                row = g * row_count + t * local_rows + r
                who = owner[row]
                whos.append(who)
                limit = jnp.minimum(cached[row] * BLK, lengths[who])
                part = dot_t(queries, cache[who, :, 0:HD])
                scores = part if r == 0 else jnp.where(row_of == r, part, scores)
                limits = jnp.full((count, 1), limit) if r == 0 else jnp.where(row_of == r, limit, limits)
            owners.append(whos)
            fresh = dot_t(queries, qland[t, :, width : width + HD])
            both.append((jnp.where(where_to < limits, scores, LOW), jnp.where(allowed, fresh, LOW)))
        for scores, fresh in both:
            highest = jnp.maximum(
                jnp.max(scores, axis=-1, keepdims=True), jnp.max(fresh, axis=-1, keepdims=True)
            )
            weights = jnp.exp2((scores - highest) * FACTOR)
            fresh_weights = jnp.exp2((fresh - highest) * FACTOR)
            total = jnp.sum(weights, axis=-1, keepdims=True)
            total = total + jnp.sum(fresh_weights, axis=-1, keepdims=True)
            weighed.append((weights, fresh_weights.astype(jnp.bfloat16), total))
        results = []
        for t, whos, (weights, fresh_weights, total) in zip(sources, owners, weighed):
            mixed = jnp.dot(
                fresh_weights,
                qland[t, :, width + HD : width + 2 * HD],
                preferred_element_type=jnp.float32,
            )
            for r in range(local_rows):
                chosen = jnp.where(row_of == r, weights, 0.0).astype(jnp.bfloat16)
                mixed = mixed + jnp.dot(
                    chosen, cache[whos[r], :, HD : 2 * HD], preferred_element_type=jnp.float32
                )
            results.append((mixed / total).astype(jnp.bfloat16))
        for t, result in zip(sources, results):
            for h in range(own_heads):
                osend[t, :, h * HD : (h + 1) * HD] = result[h * rows : (h + 1) * rows]

    def verify_some(low, high):
        def step(i, carry):
            first = low + i * VERIFY_SET
            verify_set([lax.rem(s + first + j, cycle) for j in range(VERIFY_SET)])
            for j in range(VERIFY_SET):
                @pl.when(first + j < cycle)
                def _():
                    out_copy(lax.rem(s + first + j, cycle), s).start()

            return carry

        lax.fori_loop(0, (high - low) // VERIFY_SET, step, 0)

    tile = max(1, min(group, (512 * 512) // (tokens * slots)))

    def attend(k, part, seen):
        first = k * group + part * tile
        queries = jnp.concatenate(
            [pq[:, pl.ds(pl.multiple_of((first + h) * HD, HD), HD)] for h in range(tile)], axis=0
        )
        scores = dot_t(queries, kvbuf[k, 0:seen, 0:HD]).reshape(tile, tokens, seen) + bias[:, 0:seen][None]
        highest = jnp.max(scores, axis=-1, keepdims=True)
        weights = jnp.exp2((scores - highest) * FACTOR)
        total = jnp.sum(weights, axis=-1, keepdims=True)
        mixed = jnp.dot(
            weights.astype(jnp.bfloat16).reshape(tile * tokens, seen),
            kvbuf[k, 0:seen, HD : 2 * HD],
            preferred_element_type=jnp.float32,
        )
        result = (mixed / total.reshape(tile * tokens, 1)).astype(jnp.bfloat16)
        for h in range(tile):
            obuf[:, pl.ds(pl.multiple_of((first + h) * HD, HD), HD)] = result[
                h * tokens : (h + 1) * tokens
            ]

    def prefill_piece(p):
        def wait_one(at, carry):
            side_copy(1 - y, at, p).wait_recv()
            return carry

        lax.fori_loop(0, z + y, wait_one, 0)

        parts = group // tile
        total = heads * parts
        unroll = heads if parts == 1 else 1

        def sweep(seen):
            def step(i, carry):
                for j in range(unroll):
                    at = i * unroll + j
                    attend(p * heads + at // parts, at % parts, seen)
                return carry

            lax.fori_loop(0, total // unroll, step, 0)

        @pl.when(s < cycle // 2)
        def _():
            sweep(cycle // 2 * tokens)

        @pl.when(s >= cycle // 2)
        def _():
            sweep(slots)

        piece_out(p).start()

    def piece_out(p):
        lanes = pl.ds(p * heads * group * HD, heads * group * HD)
        return pltpu.make_async_copy(obuf.at[:, lanes], pout.at[0, :, lanes], l_sem.at[p])

    forward_all(1, chain - 1)
    fetch.wait()
    forward(chain - 1, 0)
    for p in range(PIECES):
        if p + 1 < PIECES:
            forward(chain - 1, p + 1)
        prefill_piece(p)

    def rows_arrive(i, carry):
        row_copy(s, lax.rem(s + i, cycle)).wait_recv()
        return carry

    lax.fori_loop(1, cycle, rows_arrive, 0)

    def caches_arrive(t, carry):
        for i in range(1, trajs):
            group_copy(g, lax.rem(g + i, trajs), t).wait_recv()
        return carry

    lax.fori_loop(0, cycle, caches_arrive, 0)
    verify_some(1, cycle + 1)
    oland[s] = osend[s]

    def outs_arrive(i, carry):
        out_copy(s, lax.rem(s + i, cycle)).wait_recv()
        return carry

    lax.fori_loop(1, cycle, outs_arrive, 0)
    for t in range(cycle):
        block = oland[t].astype(jnp.float32)
        for r in range(local_rows):
            vout[r, :, t * width : (t + 1) * width] = block[r * steps : (r + 1) * steps].astype(
                jnp.bfloat16
            )

    for p in range(PIECES):
        piece_out(p).wait()

    def left(i, carry):
        to = lax.rem(s + i, cycle)
        head_copy(to, s).wait_send()
        row_copy(to, s).wait_send()
        out_copy(to, s).wait_send()
        return carry

    lax.fori_loop(1, cycle, left, 0)

    def left_group(t, carry):
        for i in range(1, trajs):
            group_copy(lax.rem(g + i, trajs), g, t).wait_send()
        return carry

    lax.fori_loop(0, cycle, left_group, 0)

    @pl.when(z < chain - 1)
    def _():
        def step(at, carry):
            for p in range(PIECES):
                chain_copy(at, p).wait_send()
            return carry

        lax.fori_loop(0, z + 1, step, 0)

    def left_side(at, carry):
        for p in range(PIECES):
            side_copy(y, at, p).wait_send()
        return carry

    lax.fori_loop(0, z + 1 - y, left_side, 0)


def hand_on(count, a, b, a_out, b_out, held, held_b, sems):
    size = a.shape[1] // count
    arrive = [
        pltpu.make_async_copy(
            a.at[:, pl.ds(i * size, size)], held.at[:, pl.ds(i * size, size)], sems.at[i]
        )
        for i in range(count)
    ]
    leave = [
        pltpu.make_async_copy(
            held.at[:, pl.ds(i * size, size)], a_out.at[:, pl.ds(i * size, size)], sems.at[i]
        )
        for i in range(count)
    ]
    arrive.append(pltpu.make_async_copy(b, held_b, sems.at[count]))
    leave.append(pltpu.make_async_copy(held_b, b_out, sems.at[count]))
    for copy in arrive:
        copy.start()
    for here, there in zip(arrive, leave):
        here.wait()
        there.start()
    for copy in leave:
        copy.wait()


def solution(mesh):
    cycle = mesh.shape["seq"]
    trajs = mesh.shape["group"]

    def per_device(pq, pk, pv, lengths, vq, vk, vv, owner, cached):
        tokens = pq.shape[1]
        rows = vq.shape[0] * vq.shape[1]
        width = HQ // cycle * HD
        slots = cycle * tokens
        bf16 = jnp.bfloat16
        vmem = pl.BlockSpec(memory_space=pltpu.VMEM)
        anywhere = pl.BlockSpec(memory_space=pl.ANY)
        smem = pl.BlockSpec(memory_space=pltpu.SMEM)
        dma = pltpu.SemaphoreType.DMA
        chain = cycle // 2
        outs = pl.pallas_call(
            functools.partial(kernel, cycle, trajs),
            out_shape=(
                jax.ShapeDtypeStruct(pq.shape, bf16),
                jax.ShapeDtypeStruct(vq.shape, bf16),
            ),
            in_specs=[smem] * 3 + [anywhere] + [vmem] * 5,
            out_specs=(anywhere, vmem),
            scratch_shapes=[
                pltpu.VMEM(pq.shape[1:], bf16),
                pltpu.VMEM(pq.shape[1:], bf16),
                pltpu.VMEM((HK, slots, 2 * HD), bf16),
                pltpu.VMEM((trajs, slots, 2 * HD), bf16),
                pltpu.VMEM((cycle, rows, width + 2 * HD), bf16),
                pltpu.VMEM((cycle, rows, width + 2 * HD), bf16),
                pltpu.VMEM((cycle, rows, width), bf16),
                pltpu.VMEM((cycle, rows, width), bf16),
                pltpu.VMEM((tokens, slots), jnp.float32),
                dma((PIECES + 1,)),
                dma((cycle,)), dma((cycle,)),
                dma((cycle,)), dma((cycle,)),
                dma((trajs, cycle)), dma((trajs, cycle)),
                dma((chain, PIECES)), dma((chain, PIECES)),
                dma((chain, PIECES)), dma((chain, PIECES)),
                dma((cycle,)), dma((cycle,)),
            ],
            compiler_params=pltpu.CompilerParams(
                collective_id=0, has_side_effects=True, vmem_limit_bytes=56 * 1024 * 1024
            ),
        )(lengths, owner, cached, pq, pk, pv, vq, vk, vv)
        return pl.pallas_call(
            functools.partial(hand_on, HAND),
            out_shape=(
                jax.ShapeDtypeStruct(pq.shape, bf16),
                jax.ShapeDtypeStruct(vq.shape, bf16),
            ),
            in_specs=[anywhere] * 2,
            out_specs=(anywhere, anywhere),
            scratch_shapes=[pltpu.VMEM(pq.shape, bf16), pltpu.VMEM(vq.shape, bf16), dma((HAND + 1,))],
            compiler_params=pltpu.CompilerParams(vmem_limit_bytes=60 * 1024 * 1024),
        )(*outs)

    in_specs = (
        P("group", "seq", None),
        P("group", "seq", None),
        P("group", "seq", None),
        P(),
        P(("group", "seq"), None, None),
        P(("group", "seq"), None, None),
        P(("group", "seq"), None, None),
        P(),
        P(),
    )
    out_specs = (P("group", "seq", None), P(("group", "seq"), None, None))
    return jax.shard_map(
        per_device, mesh=mesh, in_specs=in_specs, out_specs=out_specs, check_vma=False
    )
```
